32 devices in a mesh: wind: 4 (over z), state: 8 (over y, x, core).
Axes of the slice: x: 2, y: 2, z: 4, core: 2. Of those that a mesh axis runs over, the one named last changes fastest.
Arguments:
- value_next: float32 [128, 16, 256, 256], P('wind', None, 'state'), may hold values from -6 to 6
- density: float32 [128, 16, 256, 256], P('wind', None, 'state'), may hold values from 0.1 to 2
- price: float32 [128, 16], P('wind'), may hold values from -4 to 4
- wind_rate: float32 [128, 16], P('wind'), may hold values from 0.05 to 0.5
- tank_inverse: float32 [256, 256], replicated, may hold values from -0.5 to 1.5
- soc_inverse: float32 [256, 256], replicated, may hold values from -0.5 to 1.5
Outputs:
- value: float32 [128, 16, 256, 256], P('wind', None, 'state')
- density_next: float32 [128, 16, 256, 256], P('wind', None, 'state')
The draws below stay inside these ranges and needn't reach their ends.
All inputs are finite; a program needn't handle non-finite values.
Results may differ from the reference program's by a relative error of at most 0.0001.
Values sent between devices are 32-bit elements; how exact they have to be, the bound alone decides.
No kernel may reach another device: no remote copies, remote signals or barrier semaphores. Data moves between devices by JAX's collectives and lax.ppermute only.
A program may use at most 320 MiB of HBM per device.

```python
import math
import jax
import jax.numpy as jnp
from jax import lax

S = 256
K = 256
W = 128
ROOM = 16
ITERS = 4


def implicit_inverse(key, order, spread):
    first, second = jax.random.split(jax.random.fold_in(key, 17))
    diagonal = jax.random.uniform(first, (order,), jnp.float32, 0.8, 1.2)
    offdiag = jax.random.normal(second, (order, order), jnp.float32) * (spread / order ** 0.5)
    offdiag = jnp.clip(offdiag, -0.45, 0.45)
    return jnp.eye(order, dtype=jnp.float32) * diagonal[:, None] + offdiag


def draw_tank_inverse(key, part):
    spread = 0.4
    return implicit_inverse(jax.random.fold_in(key, 3), K, spread)


def draw_soc_inverse(key, part):
    spread = 0.4
    return implicit_inverse(jax.random.fold_in(key, 5), S, spread)


def block_scale(key, shape, cuts, least, top_value):
    factor_of = 1.0
    for position, blocks in cuts:
        steps = jax.random.uniform(jax.random.fold_in(jax.random.fold_in(key, 6), position), (blocks,), jnp.float32, least / len(cuts), top_value / len(cuts))
        factor_of = factor_of * jnp.repeat(jnp.exp(steps), shape[position] // blocks).reshape((-1,) + (1,) * (len(shape) - 1 - position))
    return factor_of


def normal_values(stream_key, extent, deviation, reach, cuts=(), held_as=jnp.bfloat16):
    array = jax.random.normal(stream_key, extent, jnp.float32) * deviation
    if len(cuts) > 0:
        array = block_scale(stream_key, extent, cuts, -0.22, 0.18) * array
    return jnp.clip(array, min=-reach, max=reach).astype(held_as)


def setup_inputs(seed: int = 0) -> dict:
    keys = jax.random.split(jax.random.key(seed), 7)
    return {
        "value_next": normal_values(keys[0], (W, ROOM, S, K), 1.0, 6.0, ((0, 4), (2, 8)), jnp.float32),
        "density": jnp.clip(0.1 + 1.9 * jax.random.uniform(keys[1], (W, ROOM, K, S), jnp.float32) ** block_scale(keys[1], (W, ROOM, K, S), ((0, 4), (2, 8)), -0.2, 0.2), 0.1, 2.0),
        "price": normal_values(keys[2], (W, ROOM), 1.0, 4.0, ((0, 4),), jnp.float32),
        "wind_rate": jnp.clip(jnp.exp(math.log(0.5) - 2.3025851 * jax.random.uniform(keys[3], (W, ROOM), jnp.float32) ** block_scale(keys[3], (W, ROOM), ((0, 4),), -0.2, 0.2)), 0.05, 0.5),
        "tank_inverse": draw_tank_inverse(jax.random.fold_in(keys[6], 71), 0),
        "soc_inverse": draw_soc_inverse(jax.random.fold_in(keys[6], 71), 0),
    }


step_size = 0.25
control_bound = 2.0
control_cost = 1.0
tank_spread = 0.3


def neighbours(field, axis):
    widths = [(0, 0)] * field.ndim
    widths[axis] = (1, 1)
    padded = jnp.pad(field, widths)
    length = field.shape[axis]
    upper = lax.slice_in_dim(padded, 2, length + 2, axis=axis)
    lower = lax.slice_in_dim(padded, 0, length, axis=axis)
    return upper, lower


def control_law(current, price):
    upper, lower = neighbours(current, 2)
    shifted = 0.5 * (upper - lower) + price[:, :, None, None]
    action = -control_bound * jnp.tanh(shifted / (control_cost * control_bound))
    hamilton = action * shifted + 0.5 * control_cost * action * action
    return action, hamilton


def reference(value_next, density, price, wind_rate, tank_inverse, soc_inverse):
    current = value_next
    for sweep in range(ITERS):
        action, hamilton = control_law(current, price)
        upper, lower = neighbours(current, 0)
        couple = wind_rate[:, :, None, None] * (upper + lower - 2.0 * current)
        source = value_next + step_size * (hamilton + couple)
        current = jnp.einsum("wrsk,tk->wrst", source, tank_inverse, precision=lax.Precision.HIGHEST)
    action, hamilton = control_law(current, price)
    drift = jnp.swapaxes(action, 2, 3)
    upper, lower = neighbours(drift * density, 3)
    spread = 0.5 * (upper - lower)
    tank_up, tank_down = neighbours(density, 2)
    wind_up, wind_down = neighbours(density, 0)
    tank_term = tank_spread * (tank_up + tank_down - 2.0 * density)
    wind_term = wind_rate[:, :, None, None] * (wind_up + wind_down - 2.0 * density)
    source = density + step_size * (tank_term + wind_term - spread)
    density_next = jnp.einsum("wrks,ts->wrkt", source, soc_inverse, precision=lax.Precision.HIGHEST)
    return current, density_next
```

```python
import functools

import jax
import jax.numpy as jnp
from jax import lax
from jax.experimental import pallas as pl
from jax.experimental.pallas import tpu as pltpu
from jax.sharding import PartitionSpec as P

ITERS = 4
HALO = ITERS
LANES = 128

step_size = 0.25
control_bound = 2.0
control_cost = 1.0
tank_spread = 0.3

MIB = 1 << 20


def split_parts(x):
    high = x.astype(jnp.bfloat16)
    low = (x - high.astype(jnp.float32)).astype(jnp.bfloat16)
    return high, low


def product(high, low, weight_high, weight_low):
    dot = functools.partial(jnp.dot, preferred_element_type=jnp.float32)
    return dot(high, weight_high) + (dot(low, weight_high) + dot(high, weight_low))


def half_shifted(slope4, price_half):
    return 0.25 * slope4 + price_half


def swap_groups(tiles, group):
    count = len(tiles)
    lane = lax.broadcasted_iota(jnp.int32, tiles[0].shape, len(tiles[0].shape) - 1)
    axis = len(tiles[0].shape) - 1
    bit = 1
    while bit < count:
        mine = (lane // group) & bit
        fresh = []
        for w in range(count):
            other = tiles[w ^ bit]
            if w & bit:
                rolled = pltpu.roll(other, LANES - bit * group, axis)
                fresh.append(jnp.where(mine != 0, tiles[w], rolled))
            else:
                rolled = pltpu.roll(other, bit * group, axis)
                fresh.append(jnp.where(mine == 0, tiles[w], rolled))
        tiles = fresh
        bit *= 2
    return tiles


def sweep_kernel(
    first_room, n, info, price, rate, v, wl, wr, sl, sr, tank, *rest
):
    chained = first_room > 0
    if chained:
        rest = rest[1:]
    out, sends = rest[0], rest[1 : 1 + n]
    base, field_a, field_b, x_high, x_low, t_high, t_low, stage = rest[1 + n :]
    planes, rows, cols = v.shape[0], v.shape[2], v.shape[3]
    wide = planes + 2 * HALO
    full = rows + 2 * HALO
    step = pl.program_id(0)
    room = first_room + step
    rooms = price.shape[0] // wide
    me = info[0]

    @pl.when(step == 0)
    def _():
        high, low = split_parts(tank[...])
        t_high[...] = high
        t_low[...] = low

    for p in range(wide):
        if p < HALO:
            base[p, :rows] = wl[p, 0]
        elif p < HALO + planes:
            base[p, :rows] = v[p - HALO, 0]
        else:
            base[p, :rows] = wr[p - HALO - planes, 0]
        base[p, rows : rows + HALO] = sr[p, 0]
        base[p, rows + HALO :] = sl[p, 0]

    source = base
    for sweep in range(ITERS):
        last = sweep == ITERS - 1
        begin = sweep + 1
        count = wide - 2 * begin
        kept = rows if last else full
        target = (field_a, field_b)[sweep % 2]

        def one(p, source=source, kept=kept):
            u = source[p]
            above = pltpu.roll(u, full - 1, 0)
            below = pltpu.roll(u, 1, 0)
            scalar = p * rooms + room
            y = (0.25 * (above - below))[:kept] + 0.5 * price[scalar]
            t = jnp.tanh(y)
            r = step_size * rate[scalar]
            near = source[p + 1, :kept] + source[p - 1, :kept]
            return (
                base[p, :kept]
                + t * (0.5 * t - y)
                + r * (near - 2.0 * u[:kept])
            )

        def pair(i, carry, begin=begin, one=one, kept=kept):
            p = begin + 2 * i
            both = jnp.concatenate([one(p), one(p + 1)], axis=0)
            high, low = split_parts(both)
            at = pl.ds(pl.multiple_of(i * (2 * kept), 16), 2 * kept)
            x_high[at, :] = high
            x_low[at, :] = low
            return carry

        lax.fori_loop(0, count // 2, pair, 0)
        pieces = 2
        per = (count // pieces) // 2 * 2
        done = 0
        for piece in range(pieces):
            size = per if piece < pieces - 1 else count - done
            at = pl.ds(done * kept, size * kept)
            u = product(x_high[at, :], x_low[at, :], t_high[...], t_low[...])
            u = u.reshape(size, kept, cols)
            if last:
                out[done : done + size, 0] = u
            else:
                target[begin + done : begin + done + size] = u
            done += size
        if not last:
            @pl.when(info[1] == 0)
            def _(target=target):
                target[HALO - 1] = jnp.zeros((full, cols), jnp.float32)

            @pl.when(info[2] == 0)
            def _(target=target):
                target[HALO + planes] = jnp.zeros((full, cols), jnp.float32)

            @pl.when(info[3] == 0)
            def _(target=target):
                target[:, rows + HALO :] = jnp.zeros((wide, HALO, cols), jnp.float32)

            @pl.when(info[4] == 0)
            def _(target=target):
                target[:, rows : rows + HALO] = jnp.zeros((wide, HALO, cols), jnp.float32)
        source = target

    width = cols // n
    per_tile = LANES // width

    def pack(g, carry):
        for tile in range(cols // LANES):
            at = slice(tile * LANES, (tile + 1) * LANES)
            tiles = [out[g * per_tile + w, 0, :, at] for w in range(per_tile)]
            tiles = swap_groups(tiles, width)
            for j in range(per_tile):
                stage[tile * per_tile + j, g] = tiles[j]
        return carry

    lax.fori_loop(0, planes // per_tile, pack, 0)
    for d in range(n):
        sends[d][0] = stage[jnp.bitwise_xor(me, d)]


def density_kernel(first_room, n, info, rate, dens, wl, wr, kl, kr, price_rows, soc, *rest):
    chained = first_room > 0
    takes = rest[:n]
    rest = rest[n:]
    if chained:
        rest = rest[1:]
    out = rest[0]
    column, level, x_high, x_low, g_high, g_low, m_high, m_low, q_high, q_low = rest[1:]
    planes, rows, cols = dens.shape[0], dens.shape[2], dens.shape[3]
    step = pl.program_id(0)
    room = first_room + step
    rooms = rate.shape[0] // planes
    me = info[0]
    per_tile = LANES // rows
    inner = takes[0].shape[2]

    @pl.when(step == 0)
    def _():
        m = soc[...]
        high, low = split_parts(m)
        m_high[...] = high
        m_low[...] = low
        line = lax.broadcasted_iota(jnp.int32, m.shape, 0)
        before = jnp.where(line == 0, 0.0, pltpu.roll(m, 1, 0))
        after = jnp.where(line == cols - 1, 0.0, pltpu.roll(m, cols - 1, 0))
        high, low = split_parts(step_size * (before - after))
        q_high[...] = high
        q_low[...] = low
        column[:8] = jnp.zeros((8, LANES), jnp.float32)
        column[8 + cols :] = jnp.zeros((8, LANES), jnp.float32)

    def group(g, carry):
        for d in range(n):
            at = pl.multiple_of(8 + inner * jnp.bitwise_xor(me, d), 8)
            column[pl.ds(at, inner)] = takes[d][0, g]
        y = 0.25 * (column[9 : 9 + cols] - column[7 : 7 + cols]) + 0.5 * price_rows[0, pl.ds(g, 1)]
        t = jnp.tanh(y).T
        for w in range(per_tile):
            p = g * per_tile + w
            here = dens[p, 0]
            level[8 : 8 + rows] = here
            level[7:8] = kl[0, pl.ds(p, 1)]
            level[8 + rows : 9 + rows] = kr[0, pl.ds(p, 1)]
            r = step_size * rate[p * rooms + room]
            lower = lax.max(p - 1, 0)
            upper = lax.min(p + 1, planes - 1)
            wind_low = jnp.where(p == 0, wl[0, 0], dens[lower, 0])
            wind_up = jnp.where(p == planes - 1, wr[0, 0], dens[upper, 0])
            tank = level[7 : 7 + rows] + level[9 : 9 + rows] - 2.0 * here
            x = here + (step_size * tank_spread) * tank + r * (wind_up + wind_low - 2.0 * here)
            at = pl.ds(pl.multiple_of(p * rows, 16), rows)
            high, low = split_parts(x)
            x_high[at, :] = high
            x_low[at, :] = low
            high, low = split_parts(t[w * rows : (w + 1) * rows] * here)
            g_high[at, :] = high
            g_low[at, :] = low
        return carry

    lax.fori_loop(0, planes // per_tile, group, 0)
    half = planes // 2
    for piece in range(2):
        at = pl.ds(piece * half * rows, half * rows)
        u = product(x_high[at, :], x_low[at, :], m_high[...], m_low[...])
        u += product(g_high[at, :], g_low[at, :], q_high[...], q_low[...])
        out[piece * half : (piece + 1) * half, 0] = u.reshape(half, rows, cols)


def smem():
    return pl.BlockSpec(memory_space=pltpu.SMEM)


def whole(shape):
    return pl.BlockSpec(shape, lambda i: (0,) * len(shape))


def room_block(planes, rows, cols, first=0):
    return pl.BlockSpec((planes, 1, rows, cols), lambda i: (0, first + i, 0, 0))


def run_sweeps(first, size, n, info, price, rate, value, halos, tank, previous):
    planes, rooms, rows, cols = value.shape
    wide, full = planes + 2 * HALO, rows + 2 * HALO
    groups = planes // (LANES // (cols // n))
    in_specs = [
        smem(),
        smem(),
        smem(),
        room_block(planes, rows, cols, first),
        room_block(HALO, rows, cols),
        room_block(HALO, rows, cols),
        room_block(wide, HALO, cols),
        room_block(wide, HALO, cols),
        whole((cols, cols)),
    ]
    args = [info, price, rate, value, *halos, tank]
    aliases = {}
    if first > 0:
        aliases = {len(args): 0}
        args.append(previous)
        in_specs.append(pl.BlockSpec(memory_space=pl.ANY))
    packed = jax.ShapeDtypeStruct((size, groups, rows, LANES), jnp.float32)
    most = (wide - 2) * full
    flops = size * 2 * 3 * most * ITERS * cols * cols
    return pl.pallas_call(
        functools.partial(sweep_kernel, first, n),
        grid=(size,),
        in_specs=in_specs,
        out_specs=[room_block(planes, rows, cols, first)]
        + [pl.BlockSpec((1, groups, rows, LANES), lambda i: (i, 0, 0, 0))] * n,
        out_shape=[jax.ShapeDtypeStruct(value.shape, jnp.float32)] + [packed] * n,
        scratch_shapes=[
            pltpu.VMEM((wide, full, cols), jnp.float32),
            pltpu.VMEM((wide, full, cols), jnp.float32),
            pltpu.VMEM((wide, full, cols), jnp.float32),
            pltpu.VMEM((most, cols), jnp.bfloat16),
            pltpu.VMEM((most, cols), jnp.bfloat16),
            pltpu.VMEM((cols, cols), jnp.bfloat16),
            pltpu.VMEM((cols, cols), jnp.bfloat16),
            pltpu.VMEM((n, groups, rows, LANES), jnp.float32),
        ],
        input_output_aliases=aliases,
        compiler_params=pltpu.CompilerParams(vmem_limit_bytes=40 * MIB),
        cost_estimate=pl.CostEstimate(
            flops=flops, bytes_accessed=size * planes * rows * cols * 12, transcendentals=size * most * ITERS * cols
        ),
        name="sweeps",
    )(*args)


def run_density(first, size, n, info, rate, density, halos, price_rows, soc, takes, previous):
    planes, rooms, rows, cols = density.shape
    groups = planes // (LANES // rows)
    inner = cols // n
    in_specs = [
        smem(),
        smem(),
        room_block(planes, rows, cols, first),
        room_block(1, rows, cols, first),
        room_block(1, rows, cols, first),
        pl.BlockSpec((1, planes, cols), lambda i: (first + i, 0, 0)),
        pl.BlockSpec((1, planes, cols), lambda i: (first + i, 0, 0)),
        pl.BlockSpec((1, groups, LANES), lambda i: (first + i, 0, 0)),
        whole((cols, cols)),
    ] + [pl.BlockSpec((1, groups, inner, LANES), lambda i: (i, 0, 0, 0))] * n
    args = [info, rate, density, *halos, price_rows, soc, *takes]
    aliases = {}
    if first > 0:
        aliases = {len(args): 0}
        args.append(previous)
        in_specs.append(pl.BlockSpec(memory_space=pl.ANY))
    most = planes * rows
    return pl.pallas_call(
        functools.partial(density_kernel, first, n),
        grid=(size,),
        in_specs=in_specs,
        out_specs=room_block(planes, rows, cols, first),
        out_shape=jax.ShapeDtypeStruct(density.shape, jnp.float32),
        scratch_shapes=[
            pltpu.VMEM((cols + 16, LANES), jnp.float32),
            pltpu.VMEM((rows + 16, cols), jnp.float32),
        ]
        + [pltpu.VMEM((most, cols), jnp.bfloat16)] * 4
        + [pltpu.VMEM((cols, cols), jnp.bfloat16)] * 4,
        input_output_aliases=aliases,
        compiler_params=pltpu.CompilerParams(vmem_limit_bytes=40 * MIB),
        cost_estimate=pl.CostEstimate(
            flops=size * 2 * 6 * most * cols * cols,
            bytes_accessed=size * most * cols * 12,
            transcendentals=size * most * cols,
        ),
        name="density",
    )(*args)


def neighbours(head, tail, axis):
    ends = lax.axis_size(axis) - 1
    before = lax.ppermute(tail, axis, [(i, i + 1) for i in range(ends)])
    after = lax.ppermute(head, axis, [(i + 1, i) for i in range(ends)])
    return before, after


def value_halos(value, first, size):
    planes, rooms, rows, cols = value.shape
    part = value[:, first : first + size]
    wl, wr = neighbours(part[:HALO], part[planes - HALO :], "wind")
    heads = jnp.concatenate([wl[:, :, :HALO], part[:, :, :HALO], wr[:, :, :HALO]], axis=0)
    at = rows - HALO
    tails = jnp.concatenate([wl[:, :, at:], part[:, :, at:], wr[:, :, at:]], axis=0)
    sl, sr = neighbours(heads, tails, "state")
    return wl, wr, sl, sr


def chunk_sizes(rooms):
    size = max(rooms // 8, 1)
    return [size] * (rooms // size)


def on_device(value_next, density, price, wind_rate, tank_inverse, soc_inverse):
    planes, rooms, rows, cols = value_next.shape
    n = lax.axis_size("state")
    me = lax.axis_index("state")
    at = lax.axis_index("wind")
    info = jnp.stack(
        [me, at, lax.axis_size("wind") - 1 - at, me, n - 1 - me]
    ).astype(jnp.int32)
    pair = jnp.stack([price, wind_rate])
    before, after = neighbours(pair[:, :HALO], pair[:, planes - HALO :], "wind")
    pair = jnp.concatenate([before, pair, after], axis=1)
    price_wide, rate_wide = pair[0].reshape(-1), pair[1].reshape(-1)
    tank, soc = tank_inverse.T, soc_inverse.T

    dwl, dwr = neighbours(density[:1], density[planes - 1 :], "wind")
    dkl, dkr = neighbours(
        jnp.swapaxes(density[:, :, 0], 0, 1), jnp.swapaxes(density[:, :, rows - 1], 0, 1), "state"
    )
    per_tile = LANES // rows
    price_rows = jnp.repeat(price.T.reshape(rooms, planes // per_tile, per_tile), rows, axis=2)
    rate_flat = wind_rate.reshape(-1)

    sizes = chunk_sizes(rooms)
    starts = [sum(sizes[:c]) for c in range(len(sizes))]
    value, density_next = None, None
    for first, size in zip(starts, sizes):
        halos = value_halos(value_next, first, size)
        value, *sends = run_sweeps(
            first, size, n, info, price_wide, rate_wide, value_next, halos, tank, value
        )
        takes = [sends[0]]
        for d in range(1, n):
            takes.append(lax.ppermute(sends[d], "state", [(i, i ^ d) for i in range(n)]))
        density_next = run_density(
            first, size, n, info, rate_flat, density, (dwl, dwr, dkl, dkr), price_rows, soc, takes, density_next
        )
    return value, density_next


def solution(mesh):
    field = P("wind", None, "state", None)
    placed = (field, field, P("wind", None), P("wind", None), P(), P())
    return jax.shard_map(
        on_device,
        mesh=mesh,
        in_specs=placed,
        out_specs=(field, field),
        check_vma=False,
    )
```

```python
import functools

import jax
import jax.numpy as jnp
from jax import lax
from jax.experimental import pallas as pl
from jax.experimental.pallas import tpu as pltpu
from jax.sharding import PartitionSpec as P

ITERS = 4
HALO = ITERS
LANES = 128
PIECE = 6

step_size = 0.25
control_bound = 2.0
control_cost = 1.0
tank_spread = 0.3

MIB = 1 << 20
TOKEN = jax.ShapeDtypeStruct((8, LANES), jnp.float32)


def split_parts(x):
    high = x.astype(jnp.bfloat16)
    low = (x - high.astype(jnp.float32)).astype(jnp.bfloat16)
    return high, low


def product(high, low, weight_high, weight_low):
    dot = functools.partial(jnp.dot, preferred_element_type=jnp.float32)
    return dot(high, weight_high) + (dot(low, weight_high) + dot(high, weight_low))


def half_shifted(slope4, price_half):
    return 0.25 * slope4 + price_half


def swap_groups(tiles, group):
    count = len(tiles)
    lane = lax.broadcasted_iota(jnp.int32, tiles[0].shape, len(tiles[0].shape) - 1)
    axis = len(tiles[0].shape) - 1
    bit = 1
    while bit < count:
        mine = (lane // group) & bit
        fresh = []
        for w in range(count):
            other = tiles[w ^ bit]
            if w & bit:
                rolled = pltpu.roll(other, LANES - bit * group, axis)
                fresh.append(jnp.where(mine != 0, tiles[w], rolled))
            else:
                rolled = pltpu.roll(other, bit * group, axis)
                fresh.append(jnp.where(mine == 0, tiles[w], rolled))
        tiles = fresh
        bit *= 2
    return tiles


def sweep_kernel(
    first_room, n, extra, info, price, rate, v, wl, wr, sl, sr, tank, *rest
):
    rest = rest[extra:]
    out, token, sends = rest[0], rest[1], rest[2 : 2 + n]
    base, field_a, field_b, x_high, x_low, t_high, t_low, stage = rest[2 + n :]
    token[...] = jnp.zeros(token.shape, token.dtype)
    planes, rows, cols = v.shape[0], v.shape[2], v.shape[3]
    wide = planes + 2 * HALO
    full = rows + 2 * HALO
    step = pl.program_id(0)
    room = first_room + step
    rooms = price.shape[0] // wide
    me = info[0]

    @pl.when(step == 0)
    def _():
        high, low = split_parts(tank[...])
        t_high[...] = high
        t_low[...] = low

    for p in range(wide):
        if p < HALO:
            base[p, :rows] = wl[p, 0]
        elif p < HALO + planes:
            base[p, :rows] = v[p - HALO, 0]
        else:
            base[p, :rows] = wr[p - HALO - planes, 0]
        base[p, rows : rows + HALO] = sr[p, 0]
        base[p, rows + HALO :] = sl[p, 0]

    source = base
    for sweep in range(ITERS):
        last = sweep == ITERS - 1
        begin = sweep + 1
        count = wide - 2 * begin
        kept = rows if last else full
        target = (field_a, field_b)[sweep % 2]

        def one(p, source=source, kept=kept):
            u = source[p]
            above = pltpu.roll(u, full - 1, 0)
            below = pltpu.roll(u, 1, 0)
            scalar = p * rooms + room
            y = (0.25 * (above - below))[:kept] + 0.5 * price[scalar]
            t = jnp.tanh(y)
            r = step_size * rate[scalar]
            near = source[p + 1, :kept] + source[p - 1, :kept]
            return (
                base[p, :kept]
                + t * (0.5 * t - y)
                + r * (near - 2.0 * u[:kept])
            )

        done = 0
        while done < count:
            size = min(PIECE, count - done)
            for i in range(done, done + size, 2):
                both = jnp.concatenate([one(begin + i), one(begin + i + 1)], axis=0)
                high, low = split_parts(both)
                x_high[i * kept : (i + 2) * kept] = high
                x_low[i * kept : (i + 2) * kept] = low
            at = slice(done * kept, (done + size) * kept)
            u = product(x_high[at], x_low[at], t_high[...], t_low[...])
            u = u.reshape(size, kept, cols)
            if last:
                out[done : done + size, 0] = u
            else:
                target[begin + done : begin + done + size] = u
            done += size
        if not last:
            @pl.when(info[1] == 0)
            def _(target=target):
                target[HALO - 1] = jnp.zeros((full, cols), jnp.float32)

            @pl.when(info[2] == 0)
            def _(target=target):
                target[HALO + planes] = jnp.zeros((full, cols), jnp.float32)

            @pl.when(info[3] == 0)
            def _(target=target):
                target[:, rows + HALO :] = jnp.zeros((wide, HALO, cols), jnp.float32)

            @pl.when(info[4] == 0)
            def _(target=target):
                target[:, rows : rows + HALO] = jnp.zeros((wide, HALO, cols), jnp.float32)
        source = target

    width = cols // n
    per_tile = LANES // width

    def pack(g, carry):
        for tile in range(cols // LANES):
            at = slice(tile * LANES, (tile + 1) * LANES)
            tiles = [out[g * per_tile + w, 0, :, at] for w in range(per_tile)]
            tiles = swap_groups(tiles, width)
            for j in range(per_tile):
                stage[tile * per_tile + j, g] = tiles[j]
        return carry

    lax.fori_loop(0, planes // per_tile, pack, 0, unroll=True)
    for d in range(n):
        sends[d][0] = stage[jnp.bitwise_xor(me, d)]


def density_kernel(first_room, n, extra, info, price, rate, dens, wl, wr, kl, kr, soc, *rest):
    takes = rest[:n]
    rest = rest[n + extra :]
    out, token = rest[0], rest[1]
    column, level, x_high, x_low, g_high, g_low, m_high, m_low, q_high, q_low = rest[2:]
    token[...] = jnp.zeros(token.shape, token.dtype)
    planes, rows, cols = dens.shape[0], dens.shape[2], dens.shape[3]
    step = pl.program_id(0)
    room = first_room + step
    rooms = rate.shape[0] // planes
    me = info[0]
    per_tile = LANES // rows
    inner = takes[0].shape[2]

    @pl.when(step == 0)
    def _():
        m = soc[...]
        high, low = split_parts(m)
        m_high[...] = high
        m_low[...] = low
        line = lax.broadcasted_iota(jnp.int32, m.shape, 0)
        before = jnp.where(line == 0, 0.0, pltpu.roll(m, 1, 0))
        after = jnp.where(line == cols - 1, 0.0, pltpu.roll(m, cols - 1, 0))
        high, low = split_parts(step_size * (before - after))
        q_high[...] = high
        q_low[...] = low
        column[:, :8] = jnp.zeros((2, 8, LANES), jnp.float32)
        column[:, 8 + cols :] = jnp.zeros((2, 8, LANES), jnp.float32)

    for g in range(planes // per_tile):
        for d in range(n):
            at = pl.multiple_of(8 + inner * jnp.bitwise_xor(me, d), 8)
            column[g % 2, pl.ds(at, inner)] = takes[d][0, g]
        lane = lax.broadcasted_iota(jnp.int32, (1, LANES), 1)
        half_price = jnp.zeros((1, LANES), jnp.float32)
        for w in range(per_tile):
            scalar = 0.5 * price[(g * per_tile + w) * rooms + room]
            half_price = jnp.where(lane // rows == w, scalar, half_price)
        spot = column.at[g % 2]
        y = 0.25 * (spot[9 : 9 + cols] - spot[7 : 7 + cols]) + half_price
        t = jnp.tanh(y).T
        for w in range(per_tile):
            p = g * per_tile + w
            here = dens[p, 0]
            line = level.at[w % 2]
            line[8 : 8 + rows] = here
            line[7:8] = kl[p, 0]
            line[8 + rows : 9 + rows] = kr[p, 0]
            r = step_size * rate[p * rooms + room]
            wind_low = wl[0, 0] if p == 0 else dens[p - 1, 0]
            wind_up = wr[0, 0] if p == planes - 1 else dens[p + 1, 0]
            tank = line[7 : 7 + rows] + line[9 : 9 + rows] - 2.0 * here
            x = here + (step_size * tank_spread) * tank + r * (wind_up + wind_low - 2.0 * here)
            at = slice(p * rows, (p + 1) * rows)
            high, low = split_parts(x)
            x_high[at, :] = high
            x_low[at, :] = low
            high, low = split_parts(t[w * rows : (w + 1) * rows] * here)
            g_high[at, :] = high
            g_low[at, :] = low

    half = planes // 2
    for piece in range(2):
        at = pl.ds(piece * half * rows, half * rows)
        u = product(x_high[at, :], x_low[at, :], m_high[...], m_low[...])
        u += product(g_high[at, :], g_low[at, :], q_high[...], q_low[...])
        out[piece * half : (piece + 1) * half, 0] = u.reshape(half, rows, cols)


def smem():
    return pl.BlockSpec(memory_space=pltpu.SMEM)


def whole(shape):
    return pl.BlockSpec(shape, lambda i: (0,) * len(shape))


def room_block(planes, rows, cols, first=0):
    return pl.BlockSpec((planes, 1, rows, cols), lambda i: (0, first + i, 0, 0))


def run_sweeps(first, size, n, info, price, rate, value, halos, tank, previous, after):
    planes, rooms, rows, cols = value.shape
    wide, full = planes + 2 * HALO, rows + 2 * HALO
    groups = planes // (LANES // (cols // n))
    in_specs = [
        smem(),
        smem(),
        smem(),
        room_block(planes, rows, cols, first),
        room_block(HALO, rows, cols),
        room_block(HALO, rows, cols),
        room_block(wide, HALO, cols),
        room_block(wide, HALO, cols),
        whole((cols, cols)),
    ]
    args = [info, price, rate, value, *halos, tank]
    aliases = {}
    if first > 0:
        aliases = {len(args): 0}
        args.append(previous)
        in_specs.append(pl.BlockSpec(memory_space=pl.ANY))
    in_specs += [pl.BlockSpec(memory_space=pl.ANY)] * len(after)
    extra = (first > 0) + len(after)
    args += after
    packed = jax.ShapeDtypeStruct((size, groups, rows, LANES), jnp.float32)
    most = (wide - 2) * full
    flops = size * 2 * 3 * most * ITERS * cols * cols
    return pl.pallas_call(
        functools.partial(sweep_kernel, first, n, extra),
        grid=(size,),
        in_specs=in_specs,
        out_specs=[room_block(planes, rows, cols, first), whole(TOKEN.shape)]
        + [pl.BlockSpec((1, groups, rows, LANES), lambda i: (i, 0, 0, 0))] * n,
        out_shape=[jax.ShapeDtypeStruct(value.shape, jnp.float32), TOKEN] + [packed] * n,
        scratch_shapes=[
            pltpu.VMEM((wide, full, cols), jnp.float32),
            pltpu.VMEM((wide, full, cols), jnp.float32),
            pltpu.VMEM((wide, full, cols), jnp.float32),
            pltpu.VMEM((most, cols), jnp.bfloat16),
            pltpu.VMEM((most, cols), jnp.bfloat16),
            pltpu.VMEM((cols, cols), jnp.bfloat16),
            pltpu.VMEM((cols, cols), jnp.bfloat16),
            pltpu.VMEM((n, groups, rows, LANES), jnp.float32),
        ],
        input_output_aliases=aliases,
        compiler_params=pltpu.CompilerParams(vmem_limit_bytes=40 * MIB),
        cost_estimate=pl.CostEstimate(
            flops=flops, bytes_accessed=size * planes * rows * cols * 12, transcendentals=size * most * ITERS * cols
        ),
        name="sweeps",
    )(*args)


def run_density(first, size, n, info, price, rate, density, halos, soc, takes, previous, after):
    planes, rooms, rows, cols = density.shape
    groups = planes // (LANES // rows)
    inner = cols // n
    in_specs = [
        smem(),
        smem(),
        smem(),
        room_block(planes, rows, cols, first),
        room_block(1, rows, cols, first),
        room_block(1, rows, cols, first),
        room_block(planes, 1, cols, first),
        room_block(planes, 1, cols, first),
        whole((cols, cols)),
    ] + [pl.BlockSpec((1, groups, inner, LANES), lambda i: (i, 0, 0, 0))] * n
    args = [info, price, rate, density, *halos, soc, *takes]
    aliases = {}
    if first > 0:
        aliases = {len(args): 0}
        args.append(previous)
        in_specs.append(pl.BlockSpec(memory_space=pl.ANY))
    in_specs += [pl.BlockSpec(memory_space=pl.ANY)] * len(after)
    extra = (first > 0) + len(after)
    args += after
    most = planes * rows
    return pl.pallas_call(
        functools.partial(density_kernel, first, n, extra),
        grid=(size,),
        in_specs=in_specs,
        out_specs=[room_block(planes, rows, cols, first), whole(TOKEN.shape)],
        out_shape=[jax.ShapeDtypeStruct(density.shape, jnp.float32), TOKEN],
        scratch_shapes=[
            pltpu.VMEM((2, cols + 16, LANES), jnp.float32),
            pltpu.VMEM((2, rows + 16, cols), jnp.float32),
        ]
        + [pltpu.VMEM((most, cols), jnp.bfloat16)] * 4
        + [pltpu.VMEM((cols, cols), jnp.bfloat16)] * 4,
        input_output_aliases=aliases,
        compiler_params=pltpu.CompilerParams(vmem_limit_bytes=40 * MIB),
        cost_estimate=pl.CostEstimate(
            flops=size * 2 * 6 * most * cols * cols,
            bytes_accessed=size * most * cols * 12,
            transcendentals=size * most * cols,
        ),
        name="density",
    )(*args)


def neighbours(head, tail, axis):
    ends = lax.axis_size(axis) - 1
    before = lax.ppermute(tail, axis, [(i, i + 1) for i in range(ends)])
    after = lax.ppermute(head, axis, [(i + 1, i) for i in range(ends)])
    return before, after


def held(x, token):
    return x if token is None else x + token[0, 0]


def wind_halos(value, first, size, token):
    planes = value.shape[0]
    head = held(value[:HALO, first : first + size], token)
    tail = held(value[planes - HALO :, first : first + size], token)
    return neighbours(head, tail, "wind")


def state_halos(value, wl, wr, first, size, token):
    at = value.shape[2] - HALO
    part = value[:, first : first + size]
    heads = jnp.concatenate([wl[:, :, :HALO], part[:, :, :HALO], wr[:, :, :HALO]], axis=0)
    tails = jnp.concatenate([wl[:, :, at:], part[:, :, at:], wr[:, :, at:]], axis=0)
    return neighbours(held(heads, token), held(tails, token), "state")


def chunk_sizes(rooms):
    unit = max(rooms // 8, 1)
    if rooms != 8 * unit:
        return [1] * rooms
    return [unit, 2 * unit, 2 * unit, 2 * unit, unit]


def on_device(value_next, density, price, wind_rate, tank_inverse, soc_inverse):
    planes, rooms, rows, cols = value_next.shape
    n = lax.axis_size("state")
    me = lax.axis_index("state")
    at = lax.axis_index("wind")
    info = jnp.stack(
        [me, at, lax.axis_size("wind") - 1 - at, me, n - 1 - me]
    ).astype(jnp.int32)
    sizes = chunk_sizes(rooms)
    starts = [sum(sizes[:c]) for c in range(len(sizes))]
    chunks = len(sizes)

    pair = jnp.stack([price, wind_rate])
    before, after = neighbours(pair[:, :HALO], pair[:, planes - HALO :], "wind")
    pair = jnp.concatenate([before, pair, after], axis=1)
    price_wide, rate_wide = pair[0].reshape(-1), pair[1].reshape(-1)
    price_flat, rate_flat = price.reshape(-1), wind_rate.reshape(-1)
    tank, soc = tank_inverse.T, soc_inverse.T

    winds, sweep_done, density_done, takes = {}, {}, {}, {}
    value, density_next, density_halos = None, None, None

    def step(c):
        nonlocal density_next
        density_next, density_done[c] = run_density(
            starts[c], sizes[c], n, info, price_flat, rate_flat, density, density_halos, soc, takes[c],
            density_next, [sweep_done[c + 1]] if c + 1 < chunks else [],
        )

    winds[0] = wind_halos(value_next, starts[0], sizes[0], None)
    winds[1] = wind_halos(value_next, starts[1], sizes[1], None)
    for c in range(chunks):
        first, size = starts[c], sizes[c]
        wl, wr = winds[c]
        token = sweep_done[c - 2] if c > 1 else None
        sl, sr = state_halos(value_next, wl, wr, first, size, token)
        value, sweep_done[c], *sends = run_sweeps(
            first, size, n, info, price_wide, rate_wide, value_next, (wl, wr, sl, sr), tank, value,
            [density_done[c - 2]] if c > 1 else [],
        )
        if c == 0:
            token = sweep_done[0]
            rest = sum(sizes[2:])
            wl, wr = wind_halos(value_next, starts[2], rest, token)
            for later in range(2, chunks):
                part = slice(starts[later] - starts[2], starts[later] - starts[2] + sizes[later])
                winds[later] = wl[:, part], wr[:, part]
            density_halos = neighbours(
                held(density[:1], token), held(density[planes - 1 :], token), "wind"
            ) + neighbours(
                held(density[:, :, :1], token), held(density[:, :, rows - 1 :], token), "state"
            )
        takes[c] = [sends[0]]
        for d in range(1, n):
            takes[c].append(lax.ppermute(sends[d], "state", [(i, i ^ d) for i in range(n)]))
        if c > 0:
            step(c - 1)
    step(chunks - 1)
    return value, density_next


def solution(mesh):
    field = P("wind", None, "state", None)
    placed = (field, field, P("wind", None), P("wind", None), P(), P())
    return jax.shard_map(
        on_device,
        mesh=mesh,
        in_specs=placed,
        out_specs=(field, field),
        check_vma=False,
    )
```

```python
import functools

import jax
import jax.numpy as jnp
from jax import lax
from jax.experimental import pallas as pl
from jax.experimental.pallas import tpu as pltpu
from jax.sharding import PartitionSpec as P

ITERS = 4
HALO = ITERS
LANES = 128
PIECE = 6
SHARES = (2, 3, 4, 4, 3)

step_size = 0.25
control_bound = 2.0
control_cost = 1.0
tank_spread = 0.3

MIB = 1 << 20
VMEM_LIMIT = 60 * MIB
TOKEN = jax.ShapeDtypeStruct((8, LANES), jnp.float32)


def split_parts(x):
    high = x.astype(jnp.bfloat16)
    low = (x - high.astype(jnp.float32)).astype(jnp.bfloat16)
    return high, low


def product(high, low, weight_high, weight_low):
    dot = functools.partial(jnp.dot, preferred_element_type=jnp.float32)
    return dot(high, weight_high) + (dot(low, weight_high) + dot(high, weight_low))


def half_shifted(slope4, price_half):
    return 0.25 * slope4 + price_half


def swap_groups(tiles, group):
    count = len(tiles)
    lane = lax.broadcasted_iota(jnp.int32, tiles[0].shape, len(tiles[0].shape) - 1)
    axis = len(tiles[0].shape) - 1
    bit = 1
    while bit < count:
        mine = (lane // group) & bit
        fresh = []
        for w in range(count):
            other = tiles[w ^ bit]
            if w & bit:
                rolled = pltpu.roll(other, LANES - bit * group, axis)
                fresh.append(jnp.where(mine != 0, tiles[w], rolled))
            else:
                rolled = pltpu.roll(other, bit * group, axis)
                fresh.append(jnp.where(mine == 0, tiles[w], rolled))
        tiles = fresh
        bit *= 2
    return tiles


def sweep_kernel(
    first_room, n, extra, info, price, rate, v, wl, wr, sl, sr, tank, *rest
):
    rest = rest[extra:]
    out, token, sends = rest[0], rest[1], rest[2 : 2 + n]
    base, field_a, field_b, x_high, x_low, t_high, t_low, stage = rest[2 + n :]
    token[...] = jnp.zeros(token.shape, token.dtype)
    planes, rows, cols = v.shape[0], v.shape[2], v.shape[3]
    wide = planes + 2 * HALO
    full = rows + 2 * HALO
    step = pl.program_id(0)
    room = first_room + step
    rooms = price.shape[0] // wide
    me = info[0]

    @pl.when(step == 0)
    def _():
        high, low = split_parts(tank[...])
        t_high[...] = high
        t_low[...] = low

    for p in range(HALO):
        base[p] = wl[p, 0]
        base[HALO + planes + p] = wr[p, 0]
    for p in range(planes):
        base[HALO + p, :rows] = v[p, 0]
        base[HALO + p, rows : rows + HALO] = sr[p, 0]
        base[HALO + p, rows + HALO :] = sl[p, 0]

    source = base
    for sweep in range(ITERS):
        last = sweep == ITERS - 1
        begin = sweep + 1
        count = wide - 2 * begin
        kept = rows if last else full
        target = (field_a, field_b)[sweep % 2]

        def one(p, source=source, kept=kept):
            u = source[p]
            above = pltpu.roll(u, full - 1, 0)
            below = pltpu.roll(u, 1, 0)
            scalar = p * rooms + room
            y = (0.25 * (above - below))[:kept] + 0.5 * price[scalar]
            t = jnp.tanh(y)
            r = step_size * rate[scalar]
            sides = source[p + 1, :kept] + source[p - 1, :kept]
            return (
                base[p, :kept]
                + t * (0.5 * t - y)
                + r * (sides - 2.0 * u[:kept])
            )

        done = 0
        while done < count:
            size = min(PIECE, count - done)
            for i in range(done, done + size, 2):
                both = jnp.concatenate([one(begin + i), one(begin + i + 1)], axis=0)
                high, low = split_parts(both)
                x_high[i * kept : (i + 2) * kept] = high
                x_low[i * kept : (i + 2) * kept] = low
            at = slice(done * kept, (done + size) * kept)
            u = product(x_high[at], x_low[at], t_high[...], t_low[...])
            u = u.reshape(size, kept, cols)
            if last:
                out[done : done + size, 0] = u
            else:
                target[begin + done : begin + done + size] = u
            done += size
        if not last:
            @pl.when(info[1] == 0)
            def _(target=target):
                target[HALO - 1] = jnp.zeros((full, cols), jnp.float32)

            @pl.when(info[2] == 0)
            def _(target=target):
                target[HALO + planes] = jnp.zeros((full, cols), jnp.float32)

            @pl.when(info[3] == 0)
            def _(target=target):
                target[:, rows + HALO :] = jnp.zeros((wide, HALO, cols), jnp.float32)

            @pl.when(info[4] == 0)
            def _(target=target):
                target[:, rows : rows + HALO] = jnp.zeros((wide, HALO, cols), jnp.float32)
        source = target

    width = cols // n
    per_tile = LANES // width

    def pack(g, carry):
        for tile in range(cols // LANES):
            at = slice(tile * LANES, (tile + 1) * LANES)
            tiles = [out[g * per_tile + w, 0, :, at] for w in range(per_tile)]
            tiles = swap_groups(tiles, width)
            for j in range(per_tile):
                stage[tile * per_tile + j, g] = tiles[j]
        return carry

    lax.fori_loop(0, planes // per_tile, pack, 0, unroll=True)
    for d in range(n):
        sends[d][0] = stage[jnp.bitwise_xor(me, d)]


def density_kernel(first_room, n, extra, info, price, rate, dens, wl, wr, kl, kr, soc, *rest):
    takes = rest[:n]
    rest = rest[n + extra :]
    out, token = rest[0], rest[1]
    column, level, x_high, x_low, g_high, g_low, m_high, m_low, q_high, q_low = rest[2:]
    token[...] = jnp.zeros(token.shape, token.dtype)
    planes, rows, cols = dens.shape[0], dens.shape[2], dens.shape[3]
    step = pl.program_id(0)
    room = first_room + step
    rooms = rate.shape[0] // planes
    me = info[0]
    per_tile = LANES // rows
    inner = takes[0].shape[2]

    @pl.when(step == 0)
    def _():
        m = soc[...]
        high, low = split_parts(m)
        m_high[...] = high
        m_low[...] = low
        line = lax.broadcasted_iota(jnp.int32, m.shape, 0)
        before = jnp.where(line == 0, 0.0, pltpu.roll(m, 1, 0))
        after = jnp.where(line == cols - 1, 0.0, pltpu.roll(m, cols - 1, 0))
        high, low = split_parts(step_size * (before - after))
        q_high[...] = high
        q_low[...] = low
        column[:, :8] = jnp.zeros((2, 8, LANES), jnp.float32)
        column[:, 8 + cols :] = jnp.zeros((2, 8, LANES), jnp.float32)

    for g in range(planes // per_tile):
        for d in range(n):
            at = pl.multiple_of(8 + inner * jnp.bitwise_xor(me, d), 8)
            column[g % 2, pl.ds(at, inner)] = takes[d][0, g]
        lane = lax.broadcasted_iota(jnp.int32, (1, LANES), 1)
        half_price = jnp.zeros((1, LANES), jnp.float32)
        for w in range(per_tile):
            scalar = 0.5 * price[(g * per_tile + w) * rooms + room]
            half_price = jnp.where(lane // rows == w, scalar, half_price)
        spot = column.at[g % 2]
        y = 0.25 * (spot[9 : 9 + cols] - spot[7 : 7 + cols]) + half_price
        t = jnp.tanh(y).T
        for w in range(per_tile):
            p = g * per_tile + w
            here = dens[p, 0]
            line = level.at[w % 2]
            line[8 : 8 + rows] = here
            line[7:8] = kl[p // HALO, 0, p % HALO : p % HALO + 1]
            line[8 + rows : 9 + rows] = kr[p // HALO, 0, p % HALO : p % HALO + 1]
            r = step_size * rate[p * rooms + room]
            wind_low = wl[0, 0, :rows] if p == 0 else dens[p - 1, 0]
            wind_up = wr[0, 0, :rows] if p == planes - 1 else dens[p + 1, 0]
            tank = line[7 : 7 + rows] + line[9 : 9 + rows] - 2.0 * here
            x = here + (step_size * tank_spread) * tank + r * (wind_up + wind_low - 2.0 * here)
            at = slice(p * rows, (p + 1) * rows)
            high, low = split_parts(x)
            x_high[at, :] = high
            x_low[at, :] = low
            high, low = split_parts(t[w * rows : (w + 1) * rows] * here)
            g_high[at, :] = high
            g_low[at, :] = low

    half = planes // 2
    for piece in range(2):
        at = pl.ds(piece * half * rows, half * rows)
        u = product(x_high[at, :], x_low[at, :], m_high[...], m_low[...])
        u += product(g_high[at, :], g_low[at, :], q_high[...], q_low[...])
        out[piece * half : (piece + 1) * half, 0] = u.reshape(half, rows, cols)


def smem():
    return pl.BlockSpec(memory_space=pltpu.SMEM)


def whole(shape):
    return pl.BlockSpec(shape, lambda i: (0,) * len(shape))


def room_block(planes, rows, cols, first=0):
    return pl.BlockSpec((planes, 1, rows, cols), lambda i: (0, first + i, 0, 0))


def run_sweeps(first, size, n, info, price, rate, value, halos, offsets, tank, previous, after):
    planes, rooms, rows, cols = value.shape
    wide, full = planes + 2 * HALO, rows + 2 * HALO
    groups = planes // (LANES // (cols // n))
    in_specs = [
        smem(),
        smem(),
        smem(),
        room_block(planes, rows, cols, first),
        room_block(HALO, full, cols, offsets[0]),
        room_block(HALO, full, cols, offsets[0]),
        room_block(planes, HALO, cols, offsets[1]),
        room_block(planes, HALO, cols, offsets[1]),
        whole((cols, cols)),
    ]
    args = [info, price, rate, value, *halos, tank]
    aliases = {}
    if first > 0:
        aliases = {len(args): 0}
        args.append(previous)
        in_specs.append(pl.BlockSpec(memory_space=pl.ANY))
    in_specs += [pl.BlockSpec(memory_space=pl.ANY)] * len(after)
    extra = (first > 0) + len(after)
    args += after
    packed = jax.ShapeDtypeStruct((size, groups, rows, LANES), jnp.float32)
    most = (wide - 2) * full
    flops = size * 2 * 3 * most * ITERS * cols * cols
    return pl.pallas_call(
        functools.partial(sweep_kernel, first, n, extra),
        grid=(size,),
        in_specs=in_specs,
        out_specs=[room_block(planes, rows, cols, first), whole(TOKEN.shape)]
        + [pl.BlockSpec((1, groups, rows, LANES), lambda i: (i, 0, 0, 0))] * n,
        out_shape=[jax.ShapeDtypeStruct(value.shape, jnp.float32), TOKEN] + [packed] * n,
        scratch_shapes=[
            pltpu.VMEM((wide, full, cols), jnp.float32),
            pltpu.VMEM((wide, full, cols), jnp.float32),
            pltpu.VMEM((wide, full, cols), jnp.float32),
            pltpu.VMEM((most, cols), jnp.bfloat16),
            pltpu.VMEM((most, cols), jnp.bfloat16),
            pltpu.VMEM((cols, cols), jnp.bfloat16),
            pltpu.VMEM((cols, cols), jnp.bfloat16),
            pltpu.VMEM((n, groups, rows, LANES), jnp.float32),
        ],
        input_output_aliases=aliases,
        compiler_params=pltpu.CompilerParams(vmem_limit_bytes=VMEM_LIMIT),
        cost_estimate=pl.CostEstimate(
            flops=flops, bytes_accessed=size * planes * rows * cols * 12, transcendentals=size * most * ITERS * cols
        ),
        name="sweeps",
    )(*args)


def run_density(first, size, n, info, price, rate, density, halos, offsets, soc, takes, previous, after):
    planes, rooms, rows, cols = density.shape
    groups = planes // (LANES // rows)
    inner = cols // n
    in_specs = [
        smem(),
        smem(),
        smem(),
        room_block(planes, rows, cols, first),
        pl.BlockSpec((1, 1, rows + 2 * HALO, cols), lambda i: (HALO, offsets[0] + i, 0, 0)),
        pl.BlockSpec((1, 1, rows + 2 * HALO, cols), lambda i: (HALO, offsets[0] + i, 0, 0)),
        pl.BlockSpec((planes // HALO, 1, HALO, cols), lambda i: (HALO, offsets[1] + i, 0, 0)),
        pl.BlockSpec((planes // HALO, 1, HALO, cols), lambda i: (HALO, offsets[1] + i, 0, 0)),
        whole((cols, cols)),
    ] + [pl.BlockSpec((1, groups, inner, LANES), lambda i: (i, 0, 0, 0))] * n
    args = [info, price, rate, density, *halos, soc, *takes]
    aliases = {}
    if first > 0:
        aliases = {len(args): 0}
        args.append(previous)
        in_specs.append(pl.BlockSpec(memory_space=pl.ANY))
    in_specs += [pl.BlockSpec(memory_space=pl.ANY)] * len(after)
    extra = (first > 0) + len(after)
    args += after
    most = planes * rows
    return pl.pallas_call(
        functools.partial(density_kernel, first, n, extra),
        grid=(size,),
        in_specs=in_specs,
        out_specs=[room_block(planes, rows, cols, first), whole(TOKEN.shape)],
        out_shape=[jax.ShapeDtypeStruct(density.shape, jnp.float32), TOKEN],
        scratch_shapes=[
            pltpu.VMEM((2, cols + 16, LANES), jnp.float32),
            pltpu.VMEM((2, rows + 16, cols), jnp.float32),
        ]
        + [pltpu.VMEM((most, cols), jnp.bfloat16)] * 4
        + [pltpu.VMEM((cols, cols), jnp.bfloat16)] * 4,
        input_output_aliases=aliases,
        compiler_params=pltpu.CompilerParams(vmem_limit_bytes=VMEM_LIMIT),
        cost_estimate=pl.CostEstimate(
            flops=size * 2 * 6 * most * cols * cols,
            bytes_accessed=size * most * cols * 12,
            transcendentals=size * most * cols,
        ),
        name="density",
    )(*args)


def neighbours(head, tail, axis):
    ends = lax.axis_size(axis) - 1
    before = lax.ppermute(tail, axis, [(i, i + 1) for i in range(ends)])
    after = lax.ppermute(head, axis, [(i + 1, i) for i in range(ends)])
    return before, after


def held(x, token):
    return x if token is None else x + token[0, 0]


def row_groups(edge):
    planes, rooms, cols = edge.shape
    return jnp.swapaxes(edge.reshape(planes // HALO, HALO, rooms, cols), 1, 2)


def state_halos(value, density, first, size):
    part, other = value[:, first : first + size], density[:, first : first + size]
    last = part.shape[2]
    head = jnp.concatenate([part[:, :, :HALO], row_groups(other[:, :, 0])], axis=0)
    tail = jnp.concatenate([part[:, :, last - HALO :], row_groups(other[:, :, last - 1])], axis=0)
    return neighbours(head, tail, "state")


def wind_halos(value, density, first, size, sides, token, extra=None):
    planes = value.shape[0]
    before, after = sides
    room = slice(first, first + size)
    ends = []
    for at, edge in ((slice(0, HALO), 0), (slice(planes - HALO, planes), planes - 1)):
        own = held(value[at, room], token)
        end = jnp.concatenate([own, after[at], before[at]], axis=2)
        other = jnp.pad(density[edge : edge + 1, room], ((0, 0), (0, 0), (0, 2 * HALO), (0, 0)))
        end = jnp.concatenate([end, other], axis=0)
        if extra is not None:
            end = jnp.concatenate([end, jnp.pad(extra[at], ((0, 1), (0, 0), (0, 0), (0, 0)))], axis=1)
        ends.append(end)
    return neighbours(ends[0], ends[1], "wind")


def chunk_sizes(rooms):
    shares = SHARES
    if rooms % sum(shares):
        return [1] * rooms
    return [rooms // sum(shares) * share for share in shares]


def on_device(value_next, density, price, wind_rate, tank_inverse, soc_inverse):
    planes, rooms, rows, cols = value_next.shape
    n = lax.axis_size("state")
    me = lax.axis_index("state")
    at = lax.axis_index("wind")
    info = jnp.stack(
        [me, at, lax.axis_size("wind") - 1 - at, me, n - 1 - me]
    ).astype(jnp.int32)
    sizes = chunk_sizes(rooms)
    starts = [sum(sizes[:c]) for c in range(len(sizes))]
    chunks = len(sizes)

    pair = jnp.stack([price, wind_rate], axis=1)
    slot = jnp.pad(pair[:, None], ((0, 0), (0, 0), (0, rows + 2 * HALO - 2), (0, cols - rooms)))
    price_flat, rate_flat = price.reshape(-1), wind_rate.reshape(-1)
    tank, soc = tank_inverse.T, soc_inverse.T

    sweep_done, density_done, takes = {}, {}, {}
    value, density_next = None, None

    early = sum(sizes[:2])
    later = rooms - early
    first_sides = state_halos(value_next, density, 0, early)
    later_sides = state_halos(value_next, density, early, later)

    def winds(first, size, sides, at, token, extra=None):
        sides = [x[:, at : at + size] for x in sides]
        return wind_halos(value_next, density, first, size, sides, token, extra)

    first_winds = winds(0, sizes[0], first_sides, 0, None, slot)
    wl, wr = first_winds
    wide = jnp.concatenate([wl[:HALO, sizes[0], :2, :rooms], pair, wr[:HALO, sizes[0], :2, :rooms]], axis=0)
    price_wide, rate_wide = wide[:, 0].reshape(-1), wide[:, 1].reshape(-1)
    second_winds = winds(sizes[0], sizes[1], first_sides, sizes[0], None)
    later_winds = winds(early, later, later_sides, 0, 0.0 * second_winds[0][0, 0])

    def halos_of(c):
        if c == 0:
            return first_winds + first_sides, (0, 0)
        if c == 1:
            return second_winds + first_sides, (0, sizes[0])
        return later_winds + later_sides, (starts[c] - early,) * 2

    def step(c):
        nonlocal density_next
        density_next, density_done[c] = run_density(
            starts[c], sizes[c], n, info, price_flat, rate_flat, density, *halos_of(c), soc, takes[c],
            density_next, [sweep_done[c + 1]] if c + 1 < chunks else [],
        )

    for c in range(chunks):
        first, size = starts[c], sizes[c]
        value, sweep_done[c], *sends = run_sweeps(
            first, size, n, info, price_wide, rate_wide, value_next,
            *halos_of(c), tank, value,
            [density_done[c - 2]] if c > 1 else [],
        )
        takes[c] = [sends[0]] * n
        for d in sorted(range(1, n), key=lambda d: (-(d >> 1).bit_count(), d)):
            takes[c][d] = lax.ppermute(sends[d], "state", [(i, i ^ d) for i in range(n)])
        if c > 0:
            step(c - 1)
    step(chunks - 1)
    return value, density_next


def solution(mesh):
    field = P("wind", None, "state", None)
    placed = (field, field, P("wind", None), P("wind", None), P(), P())
    return jax.shard_map(
        on_device,
        mesh=mesh,
        in_specs=placed,
        out_specs=(field, field),
        check_vma=False,
    )
```

```python
import functools

import jax
import jax.numpy as jnp
from jax import lax
from jax.experimental import pallas as pl
from jax.experimental.pallas import tpu as pltpu
from jax.sharding import PartitionSpec as P

ITERS = 4
HALO = ITERS
LANES = 128
PIECE = 6
SHARES = (2, 3, 4, 4, 3)

step_size = 0.25
control_bound = 2.0
control_cost = 1.0
tank_spread = 0.3

MIB = 1 << 20
VMEM_LIMIT = 60 * MIB
TOKEN = jax.ShapeDtypeStruct((8, LANES), jnp.float32)


def split_parts(x):
    high = x.astype(jnp.bfloat16)
    low = (x - high.astype(jnp.float32)).astype(jnp.bfloat16)
    return high, low


def product(high, low, weight_high, weight_low):
    dot = functools.partial(jnp.dot, preferred_element_type=jnp.float32)
    return dot(high, weight_high) + (dot(low, weight_high) + dot(high, weight_low))


def half_shifted(slope4, price_half):
    return 0.25 * slope4 + price_half


def swap_groups(tiles, group):
    count = len(tiles)
    lane = lax.broadcasted_iota(jnp.int32, tiles[0].shape, len(tiles[0].shape) - 1)
    axis = len(tiles[0].shape) - 1
    bit = 1
    while bit < count:
        mine = (lane // group) & bit
        fresh = []
        for w in range(count):
            other = tiles[w ^ bit]
            if w & bit:
                rolled = pltpu.roll(other, LANES - bit * group, axis)
                fresh.append(jnp.where(mine != 0, tiles[w], rolled))
            else:
                rolled = pltpu.roll(other, bit * group, axis)
                fresh.append(jnp.where(mine == 0, tiles[w], rolled))
        tiles = fresh
        bit *= 2
    return tiles


def sweep_kernel(
    first_room, n, extra, info, price, rate, v, wl, wr, sl, sr, tank, *rest
):
    rest = rest[extra:]
    out, token, sends = rest[0], rest[1], rest[2 : 2 + n]
    base, field_a, field_b, x_high, x_low, t_high, t_low, stage = rest[2 + n :]
    token[...] = jnp.zeros(token.shape, token.dtype)
    planes, rows, cols = v.shape[0], v.shape[2], v.shape[3]
    wide = planes + 2 * HALO
    full = rows + 2 * HALO
    step = pl.program_id(0)
    room = first_room + step
    rooms = price.shape[0] // wide
    me = info[0]

    @pl.when(step == 0)
    def _():
        high, low = split_parts(tank[...].T)
        t_high[...] = high
        t_low[...] = low

    for p in range(HALO):
        base[p] = wl[p, 0]
        base[HALO + planes + p] = wr[p, 0]
    for p in range(planes):
        base[HALO + p, :rows] = v[p, 0]
        base[HALO + p, rows : rows + HALO] = sr[p, 0]
        base[HALO + p, rows + HALO :] = sl[p, 0]

    source = base
    for sweep in range(ITERS):
        last = sweep == ITERS - 1
        begin = sweep + 1
        count = wide - 2 * begin
        kept = rows if last else full
        target = (field_a, field_b)[sweep % 2]

        def one(p, source=source, kept=kept):
            u = source[p]
            above = pltpu.roll(u, full - 1, 0)
            below = pltpu.roll(u, 1, 0)
            scalar = p * rooms + room
            y = (0.25 * (above - below))[:kept] + 0.5 * price[scalar]
            t = jnp.tanh(y)
            r = step_size * rate[scalar]
            sides = source[p + 1, :kept] + source[p - 1, :kept]
            return (
                base[p, :kept]
                + t * (0.5 * t - y)
                + r * (sides - 2.0 * u[:kept])
            )

        done = 0
        while done < count:
            size = min(PIECE, count - done)
            for i in range(done, done + size, 2):
                both = jnp.concatenate([one(begin + i), one(begin + i + 1)], axis=0)
                high, low = split_parts(both)
                x_high[i * kept : (i + 2) * kept] = high
                x_low[i * kept : (i + 2) * kept] = low
            at = slice(done * kept, (done + size) * kept)
            u = product(x_high[at], x_low[at], t_high[...], t_low[...])
            u = u.reshape(size, kept, cols)
            if last:
                out[done : done + size, 0] = u
            else:
                target[begin + done : begin + done + size] = u
            done += size
        if not last:
            @pl.when(info[1] == 0)
            def _(target=target):
                target[HALO - 1] = jnp.zeros((full, cols), jnp.float32)

            @pl.when(info[2] == 0)
            def _(target=target):
                target[HALO + planes] = jnp.zeros((full, cols), jnp.float32)

            @pl.when(info[3] == 0)
            def _(target=target):
                target[:, rows + HALO :] = jnp.zeros((wide, HALO, cols), jnp.float32)

            @pl.when(info[4] == 0)
            def _(target=target):
                target[:, rows : rows + HALO] = jnp.zeros((wide, HALO, cols), jnp.float32)
        source = target

    width = cols // n
    per_tile = LANES // width

    def pack(g, carry):
        for tile in range(cols // LANES):
            at = slice(tile * LANES, (tile + 1) * LANES)
            tiles = [out[g * per_tile + w, 0, :, at] for w in range(per_tile)]
            tiles = swap_groups(tiles, width)
            for j in range(per_tile):
                stage[tile * per_tile + j, g] = tiles[j]
        return carry

    lax.fori_loop(0, planes // per_tile, pack, 0, unroll=True)
    for d in range(n):
        sends[d][0] = stage[jnp.bitwise_xor(me, d)]


def density_kernel(first_room, n, extra, info, price, rate, dens, wl, wr, kl, kr, soc, *rest):
    takes = rest[:n]
    rest = rest[n + extra :]
    out, token = rest[0], rest[1]
    column, level, x_high, x_low, g_high, g_low, m_high, m_low, q_high, q_low = rest[2:]
    token[...] = jnp.zeros(token.shape, token.dtype)
    planes, rows, cols = dens.shape[0], dens.shape[2], dens.shape[3]
    step = pl.program_id(0)
    room = first_room + step
    rooms = rate.shape[0] // planes
    me = info[0]
    per_tile = LANES // rows
    inner = takes[0].shape[2]

    @pl.when(step == 0)
    def _():
        m = soc[...].T
        high, low = split_parts(m)
        m_high[...] = high
        m_low[...] = low
        line = lax.broadcasted_iota(jnp.int32, m.shape, 0)
        before = jnp.where(line == 0, 0.0, pltpu.roll(m, 1, 0))
        after = jnp.where(line == cols - 1, 0.0, pltpu.roll(m, cols - 1, 0))
        high, low = split_parts(step_size * (before - after))
        q_high[...] = high
        q_low[...] = low
        column[:, :8] = jnp.zeros((2, 8, LANES), jnp.float32)
        column[:, 8 + cols :] = jnp.zeros((2, 8, LANES), jnp.float32)

    for g in range(planes // per_tile):
        for d in range(n):
            at = pl.multiple_of(8 + inner * jnp.bitwise_xor(me, d), 8)
            column[g % 2, pl.ds(at, inner)] = takes[d][0, g]
        lane = lax.broadcasted_iota(jnp.int32, (1, LANES), 1)
        half_price = jnp.zeros((1, LANES), jnp.float32)
        for w in range(per_tile):
            scalar = 0.5 * price[(g * per_tile + w) * rooms + room]
            half_price = jnp.where(lane // rows == w, scalar, half_price)
        spot = column.at[g % 2]
        y = 0.25 * (spot[9 : 9 + cols] - spot[7 : 7 + cols]) + half_price
        t = jnp.tanh(y).T
        for w in range(per_tile):
            p = g * per_tile + w
            here = dens[p, 0]
            line = level.at[w % 2]
            line[8 : 8 + rows] = here
            line[7:8] = kl[p // HALO, 0, p % HALO : p % HALO + 1]
            line[8 + rows : 9 + rows] = kr[p // HALO, 0, p % HALO : p % HALO + 1]
            r = step_size * rate[p * rooms + room]
            wind_low = wl[0, 0, :rows] if p == 0 else dens[p - 1, 0]
            wind_up = wr[0, 0, :rows] if p == planes - 1 else dens[p + 1, 0]
            tank = line[7 : 7 + rows] + line[9 : 9 + rows] - 2.0 * here
            x = here + (step_size * tank_spread) * tank + r * (wind_up + wind_low - 2.0 * here)
            at = slice(p * rows, (p + 1) * rows)
            high, low = split_parts(x)
            x_high[at, :] = high
            x_low[at, :] = low
            high, low = split_parts(t[w * rows : (w + 1) * rows] * here)
            g_high[at, :] = high
            g_low[at, :] = low

    half = planes // 2
    for piece in range(2):
        at = pl.ds(piece * half * rows, half * rows)
        u = product(x_high[at, :], x_low[at, :], m_high[...], m_low[...])
        u += product(g_high[at, :], g_low[at, :], q_high[...], q_low[...])
        out[piece * half : (piece + 1) * half, 0] = u.reshape(half, rows, cols)


def smem():
    return pl.BlockSpec(memory_space=pltpu.SMEM)


def whole(shape):
    return pl.BlockSpec(shape, lambda i: (0,) * len(shape))


def room_block(planes, rows, cols, first=0):
    return pl.BlockSpec((planes, 1, rows, cols), lambda i: (0, first + i, 0, 0))


def run_sweeps(first, size, n, info, price, rate, value, halos, offsets, tank, previous, after):
    planes, rooms, rows, cols = value.shape
    wide, full = planes + 2 * HALO, rows + 2 * HALO
    groups = planes // (LANES // (cols // n))
    in_specs = [
        smem(),
        smem(),
        smem(),
        room_block(planes, rows, cols, first),
        room_block(HALO, full, cols, offsets[0]),
        room_block(HALO, full, cols, offsets[0]),
        room_block(planes, HALO, cols, offsets[1]),
        room_block(planes, HALO, cols, offsets[1]),
        whole((cols, cols)),
    ]
    args = [info, price, rate, value, *halos, tank]
    aliases = {}
    if first > 0:
        aliases = {len(args): 0}
        args.append(previous)
        in_specs.append(pl.BlockSpec(memory_space=pl.ANY))
    in_specs += [pl.BlockSpec(memory_space=pl.ANY)] * len(after)
    extra = (first > 0) + len(after)
    args += after
    packed = jax.ShapeDtypeStruct((size, groups, rows, LANES), jnp.float32)
    most = (wide - 2) * full
    flops = size * 2 * 3 * most * ITERS * cols * cols
    return pl.pallas_call(
        functools.partial(sweep_kernel, first, n, extra),
        grid=(size,),
        in_specs=in_specs,
        out_specs=[room_block(planes, rows, cols, first), whole(TOKEN.shape)]
        + [pl.BlockSpec((1, groups, rows, LANES), lambda i: (i, 0, 0, 0))] * n,
        out_shape=[jax.ShapeDtypeStruct(value.shape, jnp.float32), TOKEN] + [packed] * n,
        scratch_shapes=[
            pltpu.VMEM((wide, full, cols), jnp.float32),
            pltpu.VMEM((wide, full, cols), jnp.float32),
            pltpu.VMEM((wide, full, cols), jnp.float32),
            pltpu.VMEM((most, cols), jnp.bfloat16),
            pltpu.VMEM((most, cols), jnp.bfloat16),
            pltpu.VMEM((cols, cols), jnp.bfloat16),
            pltpu.VMEM((cols, cols), jnp.bfloat16),
            pltpu.VMEM((n, groups, rows, LANES), jnp.float32),
        ],
        input_output_aliases=aliases,
        compiler_params=pltpu.CompilerParams(vmem_limit_bytes=VMEM_LIMIT),
        cost_estimate=pl.CostEstimate(
            flops=flops, bytes_accessed=size * planes * rows * cols * 12, transcendentals=size * most * ITERS * cols
        ),
        name="sweeps",
    )(*args)


def run_density(first, size, n, info, price, rate, density, halos, offsets, soc, takes, previous, after):
    planes, rooms, rows, cols = density.shape
    groups = planes // (LANES // rows)
    inner = cols // n
    in_specs = [
        smem(),
        smem(),
        smem(),
        room_block(planes, rows, cols, first),
        pl.BlockSpec((1, 1, rows + 2 * HALO, cols), lambda i: (HALO, offsets[0] + i, 0, 0)),
        pl.BlockSpec((1, 1, rows + 2 * HALO, cols), lambda i: (HALO, offsets[0] + i, 0, 0)),
        pl.BlockSpec((planes // HALO, 1, HALO, cols), lambda i: (HALO, offsets[1] + i, 0, 0)),
        pl.BlockSpec((planes // HALO, 1, HALO, cols), lambda i: (HALO, offsets[1] + i, 0, 0)),
        whole((cols, cols)),
    ] + [pl.BlockSpec((1, groups, inner, LANES), lambda i: (i, 0, 0, 0))] * n
    args = [info, price, rate, density, *halos, soc, *takes]
    aliases = {}
    if first > 0:
        aliases = {len(args): 0}
        args.append(previous)
        in_specs.append(pl.BlockSpec(memory_space=pl.ANY))
    in_specs += [pl.BlockSpec(memory_space=pl.ANY)] * len(after)
    extra = (first > 0) + len(after)
    args += after
    most = planes * rows
    return pl.pallas_call(
        functools.partial(density_kernel, first, n, extra),
        grid=(size,),
        in_specs=in_specs,
        out_specs=[room_block(planes, rows, cols, first), whole(TOKEN.shape)],
        out_shape=[jax.ShapeDtypeStruct(density.shape, jnp.float32), TOKEN],
        scratch_shapes=[
            pltpu.VMEM((2, cols + 16, LANES), jnp.float32),
            pltpu.VMEM((2, rows + 16, cols), jnp.float32),
        ]
        + [pltpu.VMEM((most, cols), jnp.bfloat16)] * 4
        + [pltpu.VMEM((cols, cols), jnp.bfloat16)] * 4,
        input_output_aliases=aliases,
        compiler_params=pltpu.CompilerParams(vmem_limit_bytes=VMEM_LIMIT),
        cost_estimate=pl.CostEstimate(
            flops=size * 2 * 6 * most * cols * cols,
            bytes_accessed=size * most * cols * 12,
            transcendentals=size * most * cols,
        ),
        name="density",
    )(*args)


def neighbours(head, tail, axis):
    ends = lax.axis_size(axis) - 1
    before = lax.ppermute(tail, axis, [(i, i + 1) for i in range(ends)])
    after = lax.ppermute(head, axis, [(i + 1, i) for i in range(ends)])
    return before, after


def held(x, token):
    return x if token is None else x + token[0, 0]


def row_groups(edge):
    planes, rooms, cols = edge.shape
    return jnp.swapaxes(edge.reshape(planes // HALO, HALO, rooms, cols), 1, 2)


def state_halos(value, density, first, size):
    part, other = value[:, first : first + size], density[:, first : first + size]
    last = part.shape[2]
    head = jnp.concatenate([part[:, :, :HALO], row_groups(other[:, :, 0])], axis=0)
    tail = jnp.concatenate([part[:, :, last - HALO :], row_groups(other[:, :, last - 1])], axis=0)
    return neighbours(head, tail, "state")


def wind_halos(value, density, first, size, sides, token, extra=None):
    planes = value.shape[0]
    before, after = sides
    room = slice(first, first + size)
    ends = []
    for at, edge in ((slice(0, HALO), 0), (slice(planes - HALO, planes), planes - 1)):
        own = held(value[at, room], token)
        end = jnp.concatenate([own, after[at], before[at]], axis=2)
        other = jnp.pad(density[edge : edge + 1, room], ((0, 0), (0, 0), (0, 2 * HALO), (0, 0)))
        end = jnp.concatenate([end, other], axis=0)
        if extra is not None:
            end = jnp.concatenate([end, jnp.pad(extra[at], ((0, 1), (0, 0), (0, 0), (0, 0)))], axis=1)
        ends.append(end)
    return neighbours(ends[0], ends[1], "wind")


def chunk_sizes(rooms):
    shares = SHARES
    if rooms % sum(shares):
        return [1] * rooms
    return [rooms // sum(shares) * share for share in shares]


def on_device(value_next, density, price, wind_rate, tank_inverse, soc_inverse):
    planes, rooms, rows, cols = value_next.shape
    n = lax.axis_size("state")
    me = lax.axis_index("state")
    at = lax.axis_index("wind")
    info = jnp.stack(
        [me, at, lax.axis_size("wind") - 1 - at, me, n - 1 - me]
    ).astype(jnp.int32)
    sizes = chunk_sizes(rooms)
    starts = [sum(sizes[:c]) for c in range(len(sizes))]
    chunks = len(sizes)

    pair = jnp.stack([price, wind_rate], axis=1)
    slot = jnp.pad(pair[:, None], ((0, 0), (0, 0), (0, rows + 2 * HALO - 2), (0, cols - rooms)))
    price_flat, rate_flat = price.reshape(-1), wind_rate.reshape(-1)
    tank, soc = tank_inverse, soc_inverse

    sweep_done, density_done, takes = {}, {}, {}
    value, density_next = None, None

    early = sum(sizes[:2])
    later = rooms - early
    first_sides = state_halos(value_next, density, 0, early)
    later_sides = state_halos(value_next, density, early, later)

    def winds(first, size, sides, at, token, extra=None):
        sides = [x[:, at : at + size] for x in sides]
        return wind_halos(value_next, density, first, size, sides, token, extra)

    first_winds = winds(0, sizes[0], first_sides, 0, None, slot)
    wl, wr = first_winds
    wide = jnp.concatenate([wl[:HALO, sizes[0], :2, :rooms], pair, wr[:HALO, sizes[0], :2, :rooms]], axis=0)
    price_wide, rate_wide = wide[:, 0].reshape(-1), wide[:, 1].reshape(-1)
    second_winds = winds(sizes[0], sizes[1], first_sides, sizes[0], None)
    later_winds = winds(early, later, later_sides, 0, 0.0 * first_winds[0][0, 0])

    def halos_of(c):
        if c == 0:
            return first_winds + first_sides, (0, 0)
        if c == 1:
            return second_winds + first_sides, (0, sizes[0])
        return later_winds + later_sides, (starts[c] - early,) * 2

    def step(c):
        nonlocal density_next
        density_next, density_done[c] = run_density(
            starts[c], sizes[c], n, info, price_flat, rate_flat, density, *halos_of(c), soc, takes[c],
            density_next, [sweep_done[c + 1]] if c + 1 < chunks else [],
        )

    for c in range(chunks):
        first, size = starts[c], sizes[c]
        value, sweep_done[c], *sends = run_sweeps(
            first, size, n, info, price_wide, rate_wide, value_next,
            *halos_of(c), tank, value,
            [density_done[c - 2]] if c > 1 else [],
        )
        takes[c] = [sends[0]] * n
        for d in sorted(range(1, n), key=lambda d: (-(d >> 1).bit_count(), d)):
            takes[c][d] = lax.ppermute(sends[d], "state", [(i, i ^ d) for i in range(n)])
        if c > 0:
            step(c - 1)
    step(chunks - 1)
    return value, density_next


def solution(mesh):
    field = P("wind", None, "state", None)
    placed = (field, field, P("wind", None), P("wind", None), P(), P())
    return jax.shard_map(
        on_device,
        mesh=mesh,
        in_specs=placed,
        out_specs=(field, field),
        check_vma=False,
    )
```
